32 devices in a mesh: group: 2 (over x), tensor: 16 (over z, y, core).
Axes of the slice: x: 2, y: 2, z: 4, core: 2. Of those that a mesh axis runs over, the one named last changes fastest.
Arguments:
- tokens: bfloat16 [128, 4096], P(('group', 'tensor')), parts along dimension 0, may hold values from -6 to 6
- cotangent: bfloat16 [128, 4096], P(('group', 'tensor')), parts along dimension 0, may hold values from -6 to 6
- gate_weight: bfloat16 [4096, 16384], P(None, 'tensor'), may hold values from -0.1875 to 0.1875
- up_weight: bfloat16 [4096, 16384], P(None, 'tensor'), may hold values from -0.1875 to 0.1875
- down_weight: bfloat16 [16384, 4096], P('tensor'), may hold values from -0.09375 to 0.09375
- block_mask: int32 [3, 64, 256], P(None, None, 'tensor'), may hold values from 0 to 1, as said below
Outputs:
- mixed: bfloat16 [128, 4096], P(('group', 'tensor')), parts along dimension 0
- input_grad: bfloat16 [128, 4096], P(('group', 'tensor')), parts along dimension 0
- gate_grad: bfloat16 [4096, 32768], P(None, ('group', 'tensor')), parts along dimension 1
- up_grad: bfloat16 [4096, 32768], P(None, ('group', 'tensor')), parts along dimension 1
- down_grad: bfloat16 [32768, 4096], P(('group', 'tensor')), parts along dimension 0
The draws below stay inside these ranges and needn't reach their ends.
There are 2 independent parts, one for each index of `group`. The reference program is written for one: setup_inputs(seed, part) draws one part's arguments, and reference() takes and returns one part's arrays. A program takes and returns all parts, laid end to end along the dimension named above; an argument that names none is the same for every part. Nothing has to cross between parts.
Inputs may be any that keep to these rules, and one draw needn't show every extreme that they name: `block_mask`: each 64 x 64 block is kept (1) or dropped (0); about a quarter are kept, with the share differing from one group of 1024 hidden units to the next.
All inputs are finite; a program needn't handle non-finite values.
Results may differ from the reference program's by a relative error of at most 0.0051.
Values may be sent and summed in bfloat16 or wider, within the bound.
No kernel may reach another device: no remote copies, remote signals or barrier semaphores. Data moves between devices by JAX's collectives and lax.ppermute only.
A program may use at most 128 MiB of HBM per device.

```python
import jax
import jax.numpy as jnp

D = 4096
FF = 16384
TOKENS = 64
N_TENSOR = 16


def draw_block_mask(key, part):
    key = jax.random.fold_in(key, 11)
    level_key, flag_key = jax.random.split(key)
    columns = FF // 64 // N_TENSOR
    levels = jax.random.randint(level_key, (3, 1, N_TENSOR), 0, 7)
    limits = jnp.repeat(100 + 50 * levels, columns, axis=2)
    scores = jax.random.randint(flag_key, (3, D // 64, FF // 64), 0, 1000)
    return (scores < limits).astype(jnp.int32)


def steps_of(stream_key, shape, pieces, least, top_value):
    gain = 1.0
    for position, shards_of in pieces:
        draws = jax.random.uniform(jax.random.fold_in(jax.random.fold_in(stream_key, 6), position), (shards_of,), jnp.float32, least / len(pieces), top_value / len(pieces))
        gain = gain * jnp.repeat(jnp.exp(draws), shape[position] // shards_of).reshape((-1,) + (1,) * (len(shape) - 1 - position))
    return gain


def scatter_about(stream_key, extent, spread, bound, cuts=(), dtype=jnp.bfloat16):
    loudness = steps_of(stream_key, extent, cuts, -0.22, 0.18) if cuts else 1.0
    result = jax.random.normal(stream_key, extent, jnp.float32) * spread * loudness
    return jnp.minimum(jnp.maximum(result, -bound), bound).astype(dtype)


def setup_inputs(seed: int = 0, part: int = 0) -> dict:
    seeds = jax.random.split(jax.random.key(seed), 7)
    part_splits = jax.random.split(jax.random.fold_in(seeds[6], part), 7)
    tokens = scatter_about(part_splits[0], (TOKENS, D), 1.0, 6.0, ((0, 16),))
    cotangent = scatter_about(part_splits[1], (TOKENS, D), 1.0, 6.0, ((0, 16),))
    gate_weight = scatter_about(seeds[2], (D, FF), (D // 4) ** -0.5, 0.1875, ((1, 16),))
    up_weight = scatter_about(seeds[3], (D, FF), (D // 4) ** -0.5, 0.1875, ((1, 16),))
    down_weight = scatter_about(seeds[4], (FF, D), (FF // 4) ** -0.5, 0.09375, ((0, 16),))
    block_mask = draw_block_mask(jax.random.fold_in(seeds[6], 71), part)
    return dict(tokens=tokens, cotangent=cotangent, gate_weight=gate_weight, up_weight=up_weight, down_weight=down_weight, block_mask=block_mask)


def expand(flags):
    return jnp.repeat(jnp.repeat(flags, 64, axis=0), 64, axis=1)


def reference(tokens, cotangent, gate_weight, up_weight, down_weight, block_mask):
    keep_g = expand(block_mask[0]).astype(jnp.bfloat16)
    keep_u = expand(block_mask[1]).astype(jnp.bfloat16)
    keep_d = expand(block_mask[2]).astype(jnp.bfloat16).T
    gate_masked = gate_weight * keep_g
    up_masked = up_weight * keep_u
    down_masked = down_weight * keep_d
    gate = jnp.dot(tokens, gate_masked, preferred_element_type=jnp.float32)
    up = jnp.dot(tokens, up_masked, preferred_element_type=jnp.float32)
    sig = jax.nn.sigmoid(gate)
    act = gate * sig
    hidden = (act * up).astype(jnp.bfloat16)
    mixed = jnp.dot(hidden, down_masked, preferred_element_type=jnp.float32).astype(jnp.bfloat16)
    hidden_grad = jnp.dot(cotangent, down_masked.T, preferred_element_type=jnp.float32)
    gate_delta = (hidden_grad * up * sig * (1.0 + gate * (1.0 - sig))).astype(jnp.bfloat16)
    up_delta = (hidden_grad * act).astype(jnp.bfloat16)
    input_grad = (jnp.dot(gate_delta, gate_masked.T, preferred_element_type=jnp.float32)
                  + jnp.dot(up_delta, up_masked.T, preferred_element_type=jnp.float32)).astype(jnp.bfloat16)
    gate_grad = (jnp.dot(tokens.T, gate_delta, preferred_element_type=jnp.float32) * keep_g.astype(jnp.float32)).astype(jnp.bfloat16)
    up_grad = (jnp.dot(tokens.T, up_delta, preferred_element_type=jnp.float32) * keep_u.astype(jnp.float32)).astype(jnp.bfloat16)
    down_grad = (jnp.dot(hidden.T, cotangent, preferred_element_type=jnp.float32) * keep_d.astype(jnp.float32)).astype(jnp.bfloat16)
    return mixed, input_grad, gate_grad, up_grad, down_grad
```

```python
import functools

import jax
import jax.numpy as jnp
from jax import lax
from jax.experimental import pallas as pl
from jax.experimental.pallas import tpu as pltpu
from jax.sharding import PartitionSpec as P

AXIS = "tensor"
BLOCK = 64
BF16 = jnp.bfloat16
F32 = jnp.float32
MIB = 2**20
VMEM = pl.BlockSpec(memory_space=pltpu.VMEM)


def dot(a, b, ca=1, cb=0):
    return lax.dot_general(a, b, (((ca,), (cb,)), ((), ())), preferred_element_type=F32)


def in_vmem(x):
    return pltpu.with_memory_space_constraint(x, pltpu.VMEM)


def shape(*dims, dtype=F32):
    return jax.ShapeDtypeStruct(dims, dtype)


def params(mib):
    return pltpu.CompilerParams(vmem_limit_bytes=mib * MIB)


def cost(flops, size):
    return pl.CostEstimate(flops=flops, bytes_accessed=size, transcendentals=0)


def spread(blocks, wide):
    row = lax.broadcasted_iota(jnp.int32, (blocks, wide), 0)
    column = lax.broadcasted_iota(jnp.int32, (blocks, wide), 1)
    return (row == column // BLOCK).astype(BF16)


def mask_kernel(transposed, flags_ref, weight_ref, masked_ref, keep_ref):
    rows, columns = weight_ref.shape
    flags = flags_ref[...].astype(F32).astype(BF16)
    keep = dot(flags, spread(columns // BLOCK, columns), 0 if transposed else 1, 0)
    keep_ref[...] = keep
    keep = keep.astype(BF16)
    for block in range(rows // BLOCK):
        at = pl.ds(block * BLOCK, BLOCK)
        masked_ref[at, :] = weight_ref[at, :] * keep[block : block + 1, :]


def mask_weight(flags, weight, transposed):
    rows, columns = weight.shape
    return pl.pallas_call(
        functools.partial(mask_kernel, transposed),
        out_shape=(
            pltpu.VMEM((rows, columns), BF16),
            shape(rows // BLOCK, columns),
        ),
        in_specs=[VMEM, VMEM],
        out_specs=(VMEM, VMEM),
        input_output_aliases={1: 0},
        compiler_params=params(12),
        cost_estimate=cost(0, rows * columns),
        name="mask",
    )(flags, in_vmem(weight))


def forward_kernel(pieces, *refs):
    tokens = refs[:pieces]
    gate_ref, up_ref, down_ref = refs[pieces : pieces + 3]
    all_ref, act_ref, slope_ref, hidden_ref, hidden_t_ref, mine_ref, theirs_ref = refs[pieces + 3 :]
    all_ref[...] = jnp.concatenate([piece[...] for piece in tokens], 0)
    units = gate_ref.shape[1]
    for start in range(0, units, 256):
        at = pl.ds(start, 256)
        gate = dot(all_ref[...], gate_ref[:, at])
        up = dot(all_ref[...], up_ref[:, at])
        sig = jax.nn.sigmoid(gate)
        act = gate * sig
        act_ref[:, at] = act
        slope_ref[:, at] = up * sig * (1.0 + gate * (1.0 - sig))
        hidden = act * up
        hidden_ref[:, at] = hidden.astype(BF16)
        hidden_t_ref[at, :] = hidden.T.astype(BF16)
    half = all_ref.shape[0] // 2
    for start in range(0, down_ref.shape[1], 512):
        at = pl.ds(start, 512)
        mixed = dot(hidden_ref[...], down_ref[:, at])
        mine_ref[:, at] = mixed[:half]
        theirs_ref[:, at] = mixed[half:].astype(BF16)


def forward(tokens, gate, up, down):
    rows = sum(piece.shape[0] for piece in tokens)
    features, units = gate.shape
    return pl.pallas_call(
        functools.partial(forward_kernel, len(tokens)),
        out_shape=(
            shape(rows, features, dtype=BF16),
            shape(rows, units),
            shape(rows, units),
            shape(rows, units, dtype=BF16),
            shape(units, rows, dtype=BF16),
            shape(rows // 2, features),
            shape(rows // 2, features, dtype=BF16),
        ),
        in_specs=[VMEM] * (len(tokens) + 3),
        out_specs=(VMEM,) * 7,
        compiler_params=params(16),
        cost_estimate=cost(6 * rows * features * units, 3 * 2 * features * units),
        name="forward",
    )(*tokens, *map(in_vmem, (gate, up, down)))


def backward_kernel(pieces, *refs):
    cotangents = refs[:pieces]
    act_ref, slope_ref, gate_ref, up_ref, down_ref = refs[pieces : pieces + 5]
    all_ref, gate_delta_ref, up_delta_ref, mine_ref, theirs_ref = refs[pieces + 5 :]
    all_ref[...] = jnp.concatenate([piece[...] for piece in cotangents], 0)
    features, units = gate_ref.shape
    for start in range(0, units, 256):
        at = pl.ds(start, 256)
        hidden_grad = dot(all_ref[...], down_ref[at, :], 1, 1)
        gate_delta_ref[:, at] = (hidden_grad * slope_ref[:, at]).astype(BF16)
        up_delta_ref[:, at] = (hidden_grad * act_ref[:, at]).astype(BF16)
    half = all_ref.shape[0] // 2
    for start in range(0, features, 512):
        at = pl.ds(start, 512)
        grad = dot(gate_delta_ref[...], gate_ref[at, :], 1, 1)
        grad += dot(up_delta_ref[...], up_ref[at, :], 1, 1)
        mine_ref[:, at] = grad[:half]
        theirs_ref[:, at] = grad[half:].astype(BF16)


def backward(cotangents, act, slope, gate, up, down):
    rows = sum(piece.shape[0] for piece in cotangents)
    features, units = gate.shape
    return pl.pallas_call(
        functools.partial(backward_kernel, len(cotangents)),
        out_shape=(
            shape(rows, features, dtype=BF16),
            shape(rows, units, dtype=BF16),
            shape(rows, units, dtype=BF16),
            shape(rows // 2, features),
            shape(rows // 2, features, dtype=BF16),
        ),
        in_specs=[VMEM] * (len(cotangents) + 5),
        out_specs=(VMEM,) * 5,
        compiler_params=params(16),
        cost_estimate=cost(6 * rows * features * units, 3 * 2 * features * units),
        name="backward",
    )(*cotangents, act, slope, *map(in_vmem, (gate, up, down)))


def grads_kernel(
    tokens_ref, cotangent_ref, gate_delta_ref, up_delta_ref, hidden_t_ref, keep_g_ref, keep_u_ref, keep_d_ref,
    gate_ref, up_ref, down_ref,
):
    step = pl.program_id(0)
    blocks = gate_ref.shape[0] // BLOCK
    for delta_ref, keep_ref, out_ref in (
        (gate_delta_ref, keep_g_ref, gate_ref),
        (up_delta_ref, keep_u_ref, up_ref),
    ):
        grad = dot(tokens_ref[...], delta_ref[...], 0, 0)
        for block in range(blocks):
            keep = keep_ref[pl.ds(step * blocks + block, 1), :]
            at = slice(block * BLOCK, (block + 1) * BLOCK)
            out_ref[at, :] = (grad[at, :] * keep).astype(BF16)
    grad = dot(hidden_t_ref[...], cotangent_ref[...])
    down_ref[...] = (grad * keep_d_ref[pl.ds(step, 1), :]).astype(BF16)


def grads(tokens, cotangents, gate_delta, up_delta, hidden_t, keeps):
    rows, features = tokens.shape
    units = hidden_t.shape[0]
    steps = units // BLOCK
    wide = features // steps
    return pl.pallas_call(
        grads_kernel,
        grid=(steps,),
        out_shape=(
            shape(features, units, dtype=BF16),
            shape(features, units, dtype=BF16),
            shape(units, features, dtype=BF16),
        ),
        in_specs=[
            pl.BlockSpec((rows, wide), lambda i: (0, i)),
            VMEM,
            VMEM,
            VMEM,
            pl.BlockSpec((BLOCK, rows), lambda i: (i, 0)),
            VMEM,
            VMEM,
            VMEM,
        ],
        out_specs=(
            pl.BlockSpec((wide, units), lambda i: (i, 0)),
            pl.BlockSpec((wide, units), lambda i: (i, 0)),
            pl.BlockSpec((BLOCK, features), lambda i: (i, 0)),
        ),
        compiler_params=params(16),
        cost_estimate=cost(6 * rows * features * units, 3 * 2 * features * units),
        name="grads",
    )(tokens, cotangents, gate_delta, up_delta, hidden_t, *keeps)


def across_cores(devices):
    return [(i, i ^ 1) for i in range(devices)]


def across_chips(devices):
    def pairs(offsets):
        return [(i, ((i // 2) ^ offsets[i % 2]) * 2 + i % 2) for i in range(devices)]

    return [pairs((k + 1, k) if k else (0, 1)) for k in range(0, devices // 2, 2)]


def gather(x, devices):
    own = jnp.concatenate([x, lax.ppermute(x, AXIS, across_cores(devices))], 0)
    mine = [lax.ppermute(own, AXIS, pairs) for pairs in across_chips(devices)]
    return mine + [lax.ppermute(piece, AXIS, across_cores(devices)) for piece in mine]


def scatter(mine, theirs, devices):
    total = (mine + lax.ppermute(theirs, AXIS, across_cores(devices)).astype(F32)).astype(BF16)
    chips = across_chips(devices)
    rows = total.shape[0] // len(chips)
    parts = [lax.ppermute(total[k * rows : (k + 1) * rows], AXIS, pairs) for k, pairs in enumerate(chips)]
    part = sum(p.astype(F32) for p in parts)
    half = rows // 2
    return (part[:half] + lax.ppermute(part[half:], AXIS, across_cores(devices))).astype(BF16)


def shards(devices, tokens, cotangent, gate_weight, up_weight, down_weight, block_mask):
    gate, keep_g = mask_weight(block_mask[0], gate_weight, False)
    up, keep_u = mask_weight(block_mask[1], up_weight, False)
    down, keep_d = mask_weight(block_mask[2], down_weight, True)
    token_pieces = gather(tokens, devices)
    cotangent_pieces = gather(cotangent, devices)
    all_tokens, act, slope, _, hidden_t, mixed_mine, mixed_theirs = forward(token_pieces, gate, up, down)
    mixed = scatter(mixed_mine, mixed_theirs, devices)
    all_cotangents, gate_delta, up_delta, grad_mine, grad_theirs = backward(
        cotangent_pieces, act, slope, gate, up, down
    )
    input_grad = scatter(grad_mine, grad_theirs, devices)
    gate_grad, up_grad, down_grad = grads(
        all_tokens, all_cotangents, gate_delta, up_delta, hidden_t, (keep_g, keep_u, keep_d)
    )
    return mixed, input_grad, gate_grad, up_grad, down_grad


def solution(mesh):
    in_specs = (
        P(("group", AXIS), None),
        P(("group", AXIS), None),
        P(None, AXIS),
        P(None, AXIS),
        P(AXIS, None),
        P(None, None, AXIS),
    )
    out_specs = (
        P(("group", AXIS), None),
        P(("group", AXIS), None),
        P(None, ("group", AXIS)),
        P(None, ("group", AXIS)),
        P(("group", AXIS), None),
    )
    body = functools.partial(shards, mesh.shape[AXIS])
    return jax.shard_map(body, mesh=mesh, in_specs=in_specs, out_specs=out_specs, check_vma=False)
```

```python
import functools

import jax
import jax.numpy as jnp
from jax import lax
from jax.experimental import pallas as pl
from jax.experimental.pallas import tpu as pltpu
from jax.sharding import PartitionSpec as P

AXIS = "tensor"
BLOCK = 64
CHUNKS = 8
BF16 = jnp.bfloat16
F32 = jnp.float32
MIB = 2**20
VMEM = pl.BlockSpec(memory_space=pltpu.VMEM)


def dot(a, b, ca=1, cb=0):
    return lax.dot_general(a, b, (((ca,), (cb,)), ((), ())), preferred_element_type=F32)


def in_vmem(x):
    return pltpu.with_memory_space_constraint(x, pltpu.VMEM)


def in_hbm(x):
    return pltpu.with_memory_space_constraint(x, pltpu.HBM)


def shape(*dims, dtype=F32):
    return jax.ShapeDtypeStruct(dims, dtype)


def params(mib):
    return pltpu.CompilerParams(vmem_limit_bytes=mib * MIB)


def cost(flops, size):
    return pl.CostEstimate(flops=flops, bytes_accessed=size, transcendentals=0)


def spread(blocks, wide):
    row = lax.broadcasted_iota(jnp.int32, (blocks, wide), 0)
    column = lax.broadcasted_iota(jnp.int32, (blocks, wide), 1)
    return (row == column // BLOCK).astype(BF16)


def mask_kernel(flags_ref, *refs):
    weights, masked, keeps, sems = refs[:3], refs[3:6], refs[6:9], refs[9]
    copies = []
    for index, (weight_ref, masked_ref) in enumerate(zip(weights, masked)):
        rows = weight_ref.shape[0] // CHUNKS
        for chunk in range(CHUNKS):
            at = pl.ds(chunk * rows, rows)
            copies.append(
                pltpu.make_async_copy(weight_ref.at[at, :], masked_ref.at[at, :], sems.at[index, chunk])
            )
    for copy in copies:
        copy.start()
    for index, (masked_ref, keep_ref) in enumerate(zip(masked, keeps)):
        rows, columns = masked_ref.shape
        flags = flags_ref[index].astype(F32).astype(BF16)
        keep = dot(flags, spread(columns // BLOCK, columns), 0 if index == 2 else 1, 0)
        keep_ref[...] = keep
        keep = keep.astype(BF16)
        blocks = rows // BLOCK
        for block in range(blocks):
            if block * CHUNKS % blocks == 0:
                copies[index * CHUNKS + block * CHUNKS // blocks].wait()
            at = pl.ds(block * BLOCK, BLOCK)
            masked_ref[at, :] = masked_ref[at, :] * keep[block : block + 1, :]


def mask_weights(flags, *weights):
    hbm = pl.BlockSpec(memory_space=pltpu.HBM)
    return pl.pallas_call(
        mask_kernel,
        out_shape=tuple(pltpu.VMEM(w.shape, BF16) for w in weights)
        + tuple(shape(w.shape[0] // BLOCK, w.shape[1]) for w in weights),
        in_specs=[VMEM] + [hbm] * 3,
        out_specs=(VMEM,) * 6,
        scratch_shapes=[pltpu.SemaphoreType.DMA((3, CHUNKS))],
        compiler_params=params(8),
        cost_estimate=cost(0, sum(2 * w.size for w in weights)),
        name="mask",
    )(flags, *map(in_hbm, weights))


def layer_kernel(pieces, *refs):
    piece_refs = refs[:pieces]
    gate_ref, up_ref, down_ref = refs[pieces : pieces + 3]
    tokens_ref, cotangents_ref, gate_delta_ref, up_delta_ref, hidden_t_ref, mine_ref, theirs_ref = refs[
        pieces + 3 : pieces + 10
    ]
    hidden_ref = refs[pieces + 10]
    features, units = gate_ref.shape
    both = [piece[...] for piece in piece_refs]
    tokens_ref[...] = jnp.concatenate([piece[: piece.shape[0] // 2] for piece in both], 0)
    cotangents_ref[...] = jnp.concatenate([piece[piece.shape[0] // 2 :] for piece in both], 0)
    for start in range(0, units, 256):
        at = pl.ds(start, 256)
        gate = dot(tokens_ref[...], gate_ref[:, at])
        up = dot(tokens_ref[...], up_ref[:, at])
        hidden_grad = dot(cotangents_ref[...], down_ref[at, :], 1, 1)
        sig = jax.nn.sigmoid(gate)
        act = gate * sig
        hidden = act * up
        hidden_ref[:, at] = hidden.astype(BF16)
        hidden_t_ref[at, :] = hidden.T.astype(BF16)
        gate_delta_ref[:, at] = (hidden_grad * up * sig * (1.0 + gate * (1.0 - sig))).astype(BF16)
        up_delta_ref[:, at] = (hidden_grad * act).astype(BF16)
    half = tokens_ref.shape[0] // 2
    for start in range(0, features, 512):
        at = pl.ds(start, 512)
        mixed = dot(hidden_ref[...], down_ref[:, at])
        mine_ref[:, at] = mixed[:half]
        theirs_ref[:, at] = mixed[half:].astype(BF16)
        grad = dot(gate_delta_ref[...], gate_ref[at, :], 1, 1)
        grad += dot(up_delta_ref[...], up_ref[at, :], 1, 1)
        at = pl.ds(features + start, 512)
        mine_ref[:, at] = grad[:half]
        theirs_ref[:, at] = grad[half:].astype(BF16)


def layer(pieces, gate, up, down):
    rows = sum(piece.shape[0] for piece in pieces) // 2
    features, units = gate.shape
    return pl.pallas_call(
        functools.partial(layer_kernel, len(pieces)),
        out_shape=(
            shape(rows, features, dtype=BF16),
            shape(rows, features, dtype=BF16),
            shape(rows, units, dtype=BF16),
            shape(rows, units, dtype=BF16),
            shape(units, rows, dtype=BF16),
            shape(rows // 2, 2 * features),
            shape(rows // 2, 2 * features, dtype=BF16),
        ),
        in_specs=[VMEM] * (len(pieces) + 3),
        out_specs=(VMEM,) * 7,
        scratch_shapes=[pltpu.VMEM((rows, units), BF16)],
        compiler_params=params(16),
        cost_estimate=cost(12 * rows * features * units, 3 * 2 * features * units),
        name="layer",
    )(*pieces, *map(in_vmem, (gate, up, down)))


def grads_kernel(
    tokens_ref, cotangent_ref, gate_delta_ref, up_delta_ref, hidden_t_ref, keep_g_ref, keep_u_ref, keep_d_ref,
    gate_ref, up_ref, down_ref,
):
    step = pl.program_id(0)
    blocks = gate_ref.shape[0] // BLOCK
    for delta_ref, keep_ref, out_ref in (
        (gate_delta_ref, keep_g_ref, gate_ref),
        (up_delta_ref, keep_u_ref, up_ref),
    ):
        grad = dot(tokens_ref[...], delta_ref[...], 0, 0)
        for block in range(blocks):
            keep = keep_ref[pl.ds(step * blocks + block, 1), :]
            at = slice(block * BLOCK, (block + 1) * BLOCK)
            out_ref[at, :] = (grad[at, :] * keep).astype(BF16)
    grad = dot(hidden_t_ref[...], cotangent_ref[...])
    down_ref[...] = (grad * keep_d_ref[pl.ds(step, 1), :]).astype(BF16)


def grads(tokens, cotangents, gate_delta, up_delta, hidden_t, keeps):
    rows, features = tokens.shape
    units = hidden_t.shape[0]
    steps = units // BLOCK
    wide = features // steps
    return pl.pallas_call(
        grads_kernel,
        grid=(steps,),
        out_shape=(
            shape(features, units, dtype=BF16),
            shape(features, units, dtype=BF16),
            shape(units, features, dtype=BF16),
        ),
        in_specs=[
            pl.BlockSpec((rows, wide), lambda i: (0, i)),
            VMEM,
            VMEM,
            VMEM,
            pl.BlockSpec((BLOCK, rows), lambda i: (i, 0)),
            VMEM,
            VMEM,
            VMEM,
        ],
        out_specs=(
            pl.BlockSpec((wide, units), lambda i: (i, 0)),
            pl.BlockSpec((wide, units), lambda i: (i, 0)),
            pl.BlockSpec((BLOCK, features), lambda i: (i, 0)),
        ),
        compiler_params=params(16),
        cost_estimate=cost(6 * rows * features * units, 3 * 2 * features * units),
        name="grads",
    )(tokens, cotangents, gate_delta, up_delta, hidden_t, *keeps)


def across_cores(devices):
    return [(i, i ^ 1) for i in range(devices)]


def across_chips(devices):
    def pairs(offsets):
        return [(i, ((i // 2) ^ offsets[i % 2]) * 2 + i % 2) for i in range(devices)]

    return [pairs((k + 1, k) if k else (0, 1)) for k in range(0, devices // 2, 2)]


def gather(own, devices, after):
    mine = [lax.ppermute(own, AXIS, pairs) for pairs in across_chips(devices)]
    *mine, after = lax.optimization_barrier((*mine, after))
    return mine + [lax.ppermute(piece, AXIS, across_cores(devices)) for piece in mine], after


def scatter(total, devices, after):
    chips = across_chips(devices)
    rows = total.shape[0] // len(chips)
    parts = [lax.ppermute(total[k * rows : (k + 1) * rows], AXIS, pairs) for k, pairs in enumerate(chips)]
    *parts, after = lax.optimization_barrier((*parts, after))
    part = sum(p.astype(F32) for p in parts)
    half = rows // 2
    return (part[:half] + lax.ppermute(part[half:], AXIS, across_cores(devices))).astype(BF16), after


def shards(devices, tokens, cotangent, gate_weight, up_weight, down_weight, block_mask):
    features = tokens.shape[1]
    cores = across_cores(devices)
    own = jnp.concatenate(
        [tokens, lax.ppermute(tokens, AXIS, cores), cotangent, lax.ppermute(cotangent, AXIS, cores)], 0
    )
    own, block_mask = lax.optimization_barrier((own, block_mask))
    gate, up, down, *keeps = mask_weights(block_mask, gate_weight, up_weight, down_weight)
    pieces, keeps[0] = gather(own, devices, keeps[0])
    all_tokens, all_cotangents, gate_delta, up_delta, hidden_t, mine, theirs = layer(pieces, gate, up, down)
    total = (mine + lax.ppermute(theirs, AXIS, cores).astype(F32)).astype(BF16)
    total, hidden_t = lax.optimization_barrier((total, hidden_t))
    gate_grad, up_grad, down_grad = grads(all_tokens, all_cotangents, gate_delta, up_delta, hidden_t, keeps)
    sums, down_grad = scatter(total, devices, down_grad)
    return sums[:, :features], sums[:, features:], gate_grad, up_grad, down_grad


def solution(mesh):
    in_specs = (
        P(("group", AXIS), None),
        P(("group", AXIS), None),
        P(None, AXIS),
        P(None, AXIS),
        P(AXIS, None),
        P(None, None, AXIS),
    )
    out_specs = (
        P(("group", AXIS), None),
        P(("group", AXIS), None),
        P(None, ("group", AXIS)),
        P(None, ("group", AXIS)),
        P(("group", AXIS), None),
    )
    body = functools.partial(shards, mesh.shape[AXIS])
    return jax.shard_map(body, mesh=mesh, in_specs=in_specs, out_specs=out_specs, check_vma=False)
```

```python
import functools

import jax
import jax.numpy as jnp
from jax import lax
from jax.experimental import pallas as pl
from jax.experimental.pallas import tpu as pltpu
from jax.sharding import PartitionSpec as P

AXIS = "tensor"
BLOCK = 64
CHUNKS = 8
PARTS = 8
DOWN_PARTS = 2
BF16 = jnp.bfloat16
F32 = jnp.float32
MIB = 2**20
VMEM = pl.BlockSpec(memory_space=pltpu.VMEM)


def dot(a, b, ca=1, cb=0):
    return lax.dot_general(a, b, (((ca,), (cb,)), ((), ())), preferred_element_type=F32)


def in_vmem(x):
    return pltpu.with_memory_space_constraint(x, pltpu.VMEM)


def in_hbm(x):
    return pltpu.with_memory_space_constraint(x, pltpu.HBM)


def shape(*dims, dtype=F32):
    return jax.ShapeDtypeStruct(dims, dtype)


def params(mib):
    return pltpu.CompilerParams(vmem_limit_bytes=mib * MIB)


def cost(flops, size):
    return pl.CostEstimate(flops=flops, bytes_accessed=size, transcendentals=0)


def spread(blocks, wide):
    row = lax.broadcasted_iota(jnp.int32, (blocks, wide), 0)
    column = lax.broadcasted_iota(jnp.int32, (blocks, wide), 1)
    return (row == column // BLOCK).astype(BF16)


def keep_lanes(flags, width, transposed):
    return dot(flags, spread(width // BLOCK, width), 1 if transposed else 0, 0)


class Weight:
    def __init__(self, source, target, sems):
        chunks = min(CHUNKS, source.shape[0] // BLOCK)
        rows = source.shape[0] // chunks
        self.target = target
        self.copies = []
        for chunk in range(chunks):
            at = pl.ds(chunk * rows, rows)
            self.copies.append(pltpu.make_async_copy(source.at[at, :], target.at[at, :], sems.at[chunk]))

    def start(self):
        for copy in self.copies:
            copy.start()

    def mask(self, keep):
        keep = keep.astype(BF16)
        blocks = self.target.shape[0] // BLOCK
        each = blocks // len(self.copies)
        for block in range(blocks):
            if block % each == 0:
                self.copies[block // each].wait()
            at = pl.ds(block * BLOCK, BLOCK)
            self.target[at, :] = self.target[at, :] * keep[block : block + 1, :]


def mask_kernel(flags_ref, gate_hbm, up_hbm, down_hbm, after_ref, *refs):
    targets, keeps, sems = refs[:3], refs[3:6], refs[6]
    weights = [
        Weight(source, target, sems.at[index])
        for index, (source, target) in enumerate(zip((gate_hbm, up_hbm, down_hbm), targets))
    ]
    for weight in weights:
        weight.start()
    for index, (weight, keep_ref) in enumerate(zip(weights, keeps)):
        keep = keep_lanes(flags_ref[index], keep_ref.shape[1], index == 2)
        keep_ref[...] = keep
        weight.mask(keep)


def mask_weights(flags, weights, after):
    hbm = pl.BlockSpec(memory_space=pltpu.HBM)
    return pl.pallas_call(
        mask_kernel,
        out_shape=tuple(pltpu.VMEM(w.shape, BF16) for w in weights)
        + tuple(shape(w.shape[0] // BLOCK, w.shape[1]) for w in weights),
        in_specs=[VMEM] + [hbm] * 3 + [pl.BlockSpec(memory_space=pl.ANY)],
        out_specs=(VMEM,) * 6,
        scratch_shapes=[pltpu.SemaphoreType.DMA((3, CHUNKS))],
        compiler_params=params(8),
        cost_estimate=cost(0, sum(2 * w.size for w in weights)),
        name="mask",
    )(flags, *map(in_hbm, weights), after)


def layer_kernel(pieces, *refs):
    piece_refs = refs[:pieces]
    gate_ref, up_ref, down_ref = refs[pieces : pieces + 3]
    tokens_ref, cotangents_ref, gate_delta_ref, up_delta_ref, hidden_t_ref, mine_ref, theirs_ref = refs[
        pieces + 3 : pieces + 10
    ]
    hidden_ref = refs[pieces + 10]
    features, units = gate_ref.shape
    both = [piece[...] for piece in piece_refs]
    tokens_ref[...] = jnp.concatenate([piece[: piece.shape[0] // 2] for piece in both], 0)
    cotangents_ref[...] = jnp.concatenate([piece[piece.shape[0] // 2 :] for piece in both], 0)
    for start in range(0, units, 256):
        at = pl.ds(start, 256)
        gate = dot(tokens_ref[...], gate_ref[:, at])
        up = dot(tokens_ref[...], up_ref[:, at])
        hidden_grad = dot(cotangents_ref[...], down_ref[at, :], 1, 1)
        sig = jax.nn.sigmoid(gate)
        act = gate * sig
        hidden = act * up
        hidden_ref[:, at] = hidden.astype(BF16)
        hidden_t_ref[at, :] = hidden.T.astype(BF16)
        gate_delta_ref[:, at] = (hidden_grad * up * sig * (1.0 + gate * (1.0 - sig))).astype(BF16)
        up_delta_ref[:, at] = (hidden_grad * act).astype(BF16)
    half = tokens_ref.shape[0] // 2
    for start in range(0, features, 512):
        at = pl.ds(start, 512)
        mixed = dot(hidden_ref[...], down_ref[:, at])
        mine_ref[:, at] = mixed[:half]
        theirs_ref[:, at] = mixed[half:].astype(BF16)
        grad = dot(gate_delta_ref[...], gate_ref[at, :], 1, 1)
        grad += dot(up_delta_ref[...], up_ref[at, :], 1, 1)
        at = pl.ds(features + start, 512)
        mine_ref[:, at] = grad[:half]
        theirs_ref[:, at] = grad[half:].astype(BF16)


def layer(pieces, gate, up, down):
    rows = sum(piece.shape[0] for piece in pieces) // 2
    features, units = gate.shape
    return pl.pallas_call(
        functools.partial(layer_kernel, len(pieces)),
        out_shape=(
            shape(rows, features, dtype=BF16),
            shape(rows, features, dtype=BF16),
            shape(rows, units, dtype=BF16),
            shape(rows, units, dtype=BF16),
            shape(units, rows, dtype=BF16),
            shape(rows // 2, 2 * features),
            shape(rows // 2, 2 * features, dtype=BF16),
        ),
        in_specs=[VMEM] * (len(pieces) + 3),
        out_specs=(VMEM,) * 7,
        scratch_shapes=[pltpu.VMEM((rows, units), BF16)],
        compiler_params=params(16),
        cost_estimate=cost(12 * rows * features * units, 3 * 2 * features * units),
        name="layer",
    )(*pieces, *map(in_vmem, (gate, up, down)))


def grads_kernel(
    tokens_ref, cotangents_ref, gate_delta_ref, up_delta_ref, hidden_t_ref, keep_g_ref, keep_u_ref, keep_d_ref, after_ref,
    gate_out, up_out, down_out, gate_ref, up_ref, down_ref, sems,
):
    features, units = gate_ref.shape
    copies = []

    def send(ref, out, at):
        copies.append(pltpu.make_async_copy(ref.at[at, :], out.at[at, :], sems.at[len(copies)]))
        copies[-1].start()

    def masked(grad, keep_ref, first, columns, out_ref):
        for block in range(grad.shape[0] // BLOCK):
            keep = keep_ref[first // BLOCK + block : first // BLOCK + block + 1, columns]
            rows = grad[block * BLOCK : (block + 1) * BLOCK, :]
            out_ref[pl.ds(first + block * BLOCK, BLOCK), columns] = (rows * keep).astype(BF16)

    tall = features // PARTS
    for delta_ref, keep_ref, ref, out in (
        (gate_delta_ref, keep_g_ref, gate_ref, gate_out),
        (up_delta_ref, keep_u_ref, up_ref, up_out),
    ):
        for part in range(PARTS):
            at = pl.ds(part * tall, tall)
            masked(dot(tokens_ref[:, at], delta_ref[...], 0, 0), keep_ref, part * tall, pl.ds(0, units), ref)
            send(ref, out, at)
    flat = units // DOWN_PARTS
    for part in range(DOWN_PARTS):
        at = pl.ds(part * flat, flat)
        for start in range(0, features, 512):
            columns = pl.ds(start, 512)
            masked(dot(hidden_t_ref[at, :], cotangents_ref[:, columns]), keep_d_ref, part * flat, columns, down_ref)
        send(down_ref, down_out, at)
    for copy in copies:
        copy.wait()


def grads(tokens, cotangents, gate_delta, up_delta, hidden_t, keeps, after):
    rows, features = tokens.shape
    units = hidden_t.shape[0]
    hbm = pl.BlockSpec(memory_space=pltpu.HBM)
    shapes = ((features, units), (features, units), (units, features))
    return pl.pallas_call(
        grads_kernel,
        out_shape=tuple(shape(*dims, dtype=BF16) for dims in shapes),
        in_specs=[VMEM] * 8 + [pl.BlockSpec(memory_space=pl.ANY)],
        out_specs=(hbm,) * 3,
        scratch_shapes=[pltpu.VMEM(dims, BF16) for dims in shapes]
        + [pltpu.SemaphoreType.DMA((2 * PARTS + DOWN_PARTS,))],
        compiler_params=params(30),
        cost_estimate=cost(6 * rows * features * units, 3 * 2 * features * units),
        name="grads",
    )(tokens, cotangents, gate_delta, up_delta, hidden_t, *keeps, after)


def across_cores(devices):
    return [(i, i ^ 1) for i in range(devices)]


def across_chips(devices):
    def pairs(offsets):
        return [(i, ((i // 2) ^ offsets[i % 2]) * 2 + i % 2) for i in range(devices)]

    chips = devices // 2
    offsets = [(k + 1, k) if k else (0, 1) for k in range(0, chips, 2)]
    near = len(offsets) // 2
    return [pairs(pair) for pair in offsets[:near] + offsets[:near - 1 : -1]]


def gather(own, devices, after):
    mine = [lax.ppermute(own, AXIS, pairs) for pairs in across_chips(devices)]
    *mine, after = lax.optimization_barrier((*mine, after))
    return mine + [lax.ppermute(piece, AXIS, across_cores(devices)) for piece in mine], after


def scatter(total, devices, after):
    chips = across_chips(devices)
    rows = total.shape[0] // len(chips)
    parts = [lax.ppermute(total[k * rows : (k + 1) * rows], AXIS, pairs) for k, pairs in enumerate(chips)]
    *parts, after = lax.optimization_barrier((*parts, after))
    part = sum(p.astype(F32) for p in parts)
    half = rows // 2
    return (part[:half] + lax.ppermute(part[half:], AXIS, across_cores(devices))).astype(BF16), after


def shards(devices, tokens, cotangent, gate_weight, up_weight, down_weight, block_mask):
    features = tokens.shape[1]
    cores = across_cores(devices)
    here = lax.optimization_barrier(jnp.concatenate([tokens, cotangent], 0))
    flags = jnp.swapaxes(block_mask, 1, 2).astype(BF16)
    other = lax.ppermute(tokens, AXIS, cores), lax.ppermute(cotangent, AXIS, cores)
    here, flags, other = lax.optimization_barrier((here, flags, other))
    rows = tokens.shape[0]
    own = jnp.concatenate([here[:rows], other[0], here[rows:], other[1]], 0)
    gate, up, down, *keeps = mask_weights(flags, (gate_weight, up_weight, down_weight), own)
    pieces, keeps[0] = gather(own, devices, keeps[0])
    all_tokens, all_cotangents, gate_delta, up_delta, hidden_t, mine, theirs = layer(pieces, gate, up, down)
    total = (mine + lax.ppermute(theirs, AXIS, cores).astype(F32)).astype(BF16)
    gate_grad, up_grad, down_grad = grads(
        all_tokens, all_cotangents, gate_delta, up_delta, hidden_t, keeps, total
    )
    sums, down_grad = scatter(total, devices, down_grad)
    return sums[:, :features], sums[:, features:], gate_grad, up_grad, down_grad


def solution(mesh):
    in_specs = (
        P(("group", AXIS), None),
        P(("group", AXIS), None),
        P(None, AXIS),
        P(None, AXIS),
        P(AXIS, None),
        P(None, None, AXIS),
    )
    out_specs = (
        P(("group", AXIS), None),
        P(("group", AXIS), None),
        P(None, ("group", AXIS)),
        P(None, ("group", AXIS)),
        P(("group", AXIS), None),
    )
    body = functools.partial(shards, mesh.shape[AXIS])
    return jax.shard_map(body, mesh=mesh, in_specs=in_specs, out_specs=out_specs, check_vma=False)
```

```python
import functools

import jax
import jax.numpy as jnp
from jax import lax
from jax.experimental import pallas as pl
from jax.experimental.pallas import tpu as pltpu
from jax.sharding import PartitionSpec as P

AXIS = "tensor"
BLOCK = 64
CHUNKS = 8
PARTS = 8
SLOTS = 10
BF16 = jnp.bfloat16
F32 = jnp.float32
MIB = 2**20
VMEM = pl.BlockSpec(memory_space=pltpu.VMEM)


def dot(a, b, ca=1, cb=0):
    return lax.dot_general(a, b, (((ca,), (cb,)), ((), ())), preferred_element_type=F32)


def in_vmem(x):
    return pltpu.with_memory_space_constraint(x, pltpu.VMEM)


def in_hbm(x):
    return pltpu.with_memory_space_constraint(x, pltpu.HBM)


def shape(*dims, dtype=F32):
    return jax.ShapeDtypeStruct(dims, dtype)


def params(mib):
    return pltpu.CompilerParams(vmem_limit_bytes=mib * MIB)


def cost(flops, size):
    return pl.CostEstimate(flops=flops, bytes_accessed=size, transcendentals=0)


def spread(blocks, wide):
    row = lax.broadcasted_iota(jnp.int32, (blocks, wide), 0)
    column = lax.broadcasted_iota(jnp.int32, (blocks, wide), 1)
    return (row == column // BLOCK).astype(BF16)


def keep_lanes(flags, width, transposed):
    return dot(flags, spread(width // BLOCK, width), 1 if transposed else 0, 0)


class Weight:
    def __init__(self, source, target, sems):
        chunks = min(CHUNKS, source.shape[0] // BLOCK)
        rows = source.shape[0] // chunks
        self.target = target
        self.copies = []
        for chunk in range(chunks):
            at = pl.ds(chunk * rows, rows)
            self.copies.append(pltpu.make_async_copy(source.at[at, :], target.at[at, :], sems.at[chunk]))

    def start(self):
        for copy in self.copies:
            copy.start()

    def mask(self, keep, transposed=None):
        keep = keep.astype(BF16)
        blocks = self.target.shape[0] // BLOCK
        each = blocks // len(self.copies)
        for block in range(blocks):
            if block % each == 0:
                self.copies[block // each].wait()
            at = pl.ds(block * BLOCK, BLOCK)
            self.target[at, :] = self.target[at, :] * keep[block : block + 1, :]
            if transposed is not None and block % 2:
                pair = pl.ds((block - 1) * BLOCK, 2 * BLOCK)
                transposed[:, pair] = self.target[pair, :].T


def mask_kernel(flags_ref, gate_hbm, up_hbm, down_hbm, after_ref, *refs):
    targets, transposed, keeps, sems = refs[:3], (*refs[3:5], None), refs[5:8], refs[8]
    weights = [
        Weight(source, target, sems.at[index])
        for index, (source, target) in enumerate(zip((gate_hbm, up_hbm, down_hbm), targets))
    ]
    for weight in weights:
        weight.start()
    for index, (weight, keep_ref) in enumerate(zip(weights, keeps)):
        keep = keep_lanes(flags_ref[index], keep_ref.shape[1], index == 2)
        keep_ref[...] = keep
        weight.mask(keep, transposed[index])


def mask_weights(flags, weights, after):
    hbm = pl.BlockSpec(memory_space=pltpu.HBM)
    return pl.pallas_call(
        mask_kernel,
        out_shape=tuple(pltpu.VMEM(w.shape, BF16) for w in weights)
        + tuple(pltpu.VMEM(w.shape[::-1], BF16) for w in weights[:2])
        + tuple(shape(w.shape[0] // BLOCK, w.shape[1]) for w in weights),
        in_specs=[VMEM] + [hbm] * 3 + [pl.BlockSpec(memory_space=pl.ANY)],
        out_specs=(VMEM,) * 8,
        scratch_shapes=[pltpu.SemaphoreType.DMA((3, CHUNKS))],
        compiler_params=params(8),
        cost_estimate=cost(0, sum(2 * w.size for w in weights)),
        name="mask",
    )(flags, *map(in_hbm, weights), after)


def layer_kernel(pieces, *refs):
    piece_refs = refs[:pieces]
    gate_ref, up_ref, down_ref, gate_t_ref, up_t_ref = refs[pieces : pieces + 5]
    tokens_ref, cotangents_ref, gate_delta_ref, up_delta_ref, hidden_t_ref, mine_ref, theirs_ref = refs[
        pieces + 5 : pieces + 12
    ]
    hidden_ref = refs[pieces + 12]
    features, units = gate_ref.shape
    both = [piece[...] for piece in piece_refs]
    tokens_ref[...] = jnp.concatenate([piece[: piece.shape[0] // 2] for piece in both], 0)
    cotangents_ref[...] = jnp.concatenate([piece[piece.shape[0] // 2 :] for piece in both], 0)
    for start in range(0, units, 256):
        at = pl.ds(start, 256)
        gate = dot(tokens_ref[...], gate_ref[:, at])
        up = dot(tokens_ref[...], up_ref[:, at])
        hidden_grad = dot(cotangents_ref[...], down_ref[at, :], 1, 1)
        sig = jax.nn.sigmoid(gate)
        act = gate * sig
        hidden = act * up
        hidden_ref[:, at] = hidden.astype(BF16)
        hidden_t_ref[at, :] = hidden.T.astype(BF16)
        gate_delta_ref[:, at] = (hidden_grad * up * sig * (1.0 + gate * (1.0 - sig))).astype(BF16)
        up_delta_ref[:, at] = (hidden_grad * act).astype(BF16)
    half = tokens_ref.shape[0] // 2
    for start in range(0, features, 512):
        at = pl.ds(start, 512)
        mixed = dot(hidden_ref[...], down_ref[:, at])
        mine_ref[:, at] = mixed[:half]
        theirs_ref[:, at] = mixed[half:].astype(BF16)
        grad = dot(gate_delta_ref[...], gate_t_ref[:, at])
        grad += dot(up_delta_ref[...], up_t_ref[:, at])
        at = pl.ds(features + start, 512)
        mine_ref[:, at] = grad[:half]
        theirs_ref[:, at] = grad[half:].astype(BF16)


def layer(pieces, gate, up, down, gate_t, up_t):
    rows = sum(piece.shape[0] for piece in pieces) // 2
    features, units = gate.shape
    return pl.pallas_call(
        functools.partial(layer_kernel, len(pieces)),
        out_shape=(
            shape(rows, features, dtype=BF16),
            shape(rows, features, dtype=BF16),
            shape(rows, units, dtype=BF16),
            shape(rows, units, dtype=BF16),
            shape(units, rows, dtype=BF16),
            shape(rows // 2, 2 * features),
            shape(rows // 2, 2 * features, dtype=BF16),
        ),
        in_specs=[VMEM] * (len(pieces) + 5),
        out_specs=(VMEM,) * 7,
        scratch_shapes=[pltpu.VMEM((rows, units), BF16)],
        compiler_params=params(8),
        cost_estimate=cost(12 * rows * features * units, 3 * 2 * features * units),
        name="layer",
    )(*pieces, *map(in_vmem, (gate, up, down, gate_t, up_t)))


def grads_kernel(
    tokens_ref, cotangents_ref, gate_delta_ref, up_delta_ref, hidden_t_ref, keep_g_ref, keep_u_ref, keep_d_ref, after_ref,
    gate_out, up_out, down_out, ring_ref, sems,
):
    features, units = gate_out.shape
    slots, tall, _ = ring_ref.shape
    copies = []

    def slot(rows):
        count = len(copies)
        if count >= slots and count % 2 == 0:
            copies[count - slots].wait()
            copies[count - slots + 1].wait()
        return ring_ref.at[count % slots, pl.ds(0, rows), :]

    def fill(part_ref, columns, grad, keep):
        for block in range(grad.shape[0] // BLOCK):
            at = slice(block * BLOCK, (block + 1) * BLOCK)
            part_ref[at, columns] = (grad[at, :] * keep[block : block + 1, :]).astype(BF16)

    def send(part_ref, out):
        copies.append(pltpu.make_async_copy(part_ref, out, sems.at[len(copies)]))
        copies[-1].start()

    for delta_ref, keep_ref, out in ((gate_delta_ref, keep_g_ref, gate_out), (up_delta_ref, keep_u_ref, up_out)):
        for first in range(0, features, tall):
            at = pl.ds(first, tall)
            part_ref = slot(tall)
            grad = dot(tokens_ref[:, at], delta_ref[...], 0, 0)
            fill(part_ref, slice(0, units), grad, keep_ref[pl.ds(first // BLOCK, tall // BLOCK), :])
            send(part_ref, out.at[at, :])
    flat = min(tall, units)
    wide = min(512, units)
    for first in range(0, units, flat):
        at = pl.ds(first, flat)
        for left in range(0, features, units):
            part_ref = slot(flat)
            for start in range(0, units, wide):
                columns = pl.ds(left + start, wide)
                grad = dot(hidden_t_ref[at, :], cotangents_ref[:, columns])
                keep = keep_d_ref[pl.ds(first // BLOCK, flat // BLOCK), columns]
                fill(part_ref, slice(start, start + wide), grad, keep)
            send(part_ref, down_out.at[at, pl.ds(left, units)])
    for copy in copies[-slots:]:
        copy.wait()


def grads(tokens, cotangents, gate_delta, up_delta, hidden_t, keeps, after):
    rows, features = tokens.shape
    units = hidden_t.shape[0]
    tall = features // PARTS
    hbm = pl.BlockSpec(memory_space=pltpu.HBM)
    shapes = ((features, units), (features, units), (units, features))
    return pl.pallas_call(
        grads_kernel,
        out_shape=tuple(shape(*dims, dtype=BF16) for dims in shapes),
        in_specs=[VMEM] * 8 + [pl.BlockSpec(memory_space=pl.ANY)],
        out_specs=(hbm,) * 3,
        scratch_shapes=[
            pltpu.VMEM((SLOTS, tall, units), BF16),
            pltpu.SemaphoreType.DMA((2 * PARTS + features // min(tall, units),)),
        ],
        compiler_params=params(11),
        cost_estimate=cost(6 * rows * features * units, 3 * 2 * features * units),
        name="grads",
    )(tokens, cotangents, gate_delta, up_delta, hidden_t, *keeps, after)


def across_cores(devices):
    return [(i, i ^ 1) for i in range(devices)]


def across_chips(devices):
    def pairs(offsets):
        return [(i, ((i // 2) ^ offsets[i % 2]) * 2 + i % 2) for i in range(devices)]

    chips = devices // 2
    offsets = [(k + 1, k) if k else (0, 1) for k in range(0, chips, 2)]
    near = len(offsets) // 2
    return [pairs(pair) for pair in offsets[:near] + offsets[:near - 1 : -1]]


def gather(own, devices, after):
    mine = [lax.ppermute(own, AXIS, pairs) for pairs in across_chips(devices)]
    *mine, after = lax.optimization_barrier((*mine, after))
    return mine + [lax.ppermute(piece, AXIS, across_cores(devices)) for piece in mine], after


def scatter(total, devices, after):
    chips = across_chips(devices)
    rows = total.shape[0] // len(chips)
    parts = [lax.ppermute(total[k * rows : (k + 1) * rows], AXIS, pairs) for k, pairs in enumerate(chips)]
    *parts, after = lax.optimization_barrier((*parts, after))
    part = sum(p.astype(F32) for p in parts)
    half = rows // 2
    return (part[:half] + lax.ppermute(part[half:], AXIS, across_cores(devices))).astype(BF16), after


def shards(devices, tokens, cotangent, gate_weight, up_weight, down_weight, block_mask):
    features = tokens.shape[1]
    cores = across_cores(devices)
    here = lax.optimization_barrier(jnp.concatenate([tokens, cotangent], 0))
    flags = jnp.swapaxes(block_mask, 1, 2).astype(BF16)
    other = lax.ppermute(tokens, AXIS, cores), lax.ppermute(cotangent, AXIS, cores)
    here, flags, other = lax.optimization_barrier((here, flags, other))
    rows = tokens.shape[0]
    own = jnp.concatenate([here[:rows], other[0], here[rows:], other[1]], 0)
    gate, up, down, gate_t, up_t, *keeps = mask_weights(flags, (gate_weight, up_weight, down_weight), own)
    pieces, keeps[0] = gather(own, devices, keeps[0])
    all_tokens, all_cotangents, gate_delta, up_delta, hidden_t, mine, theirs = layer(
        pieces, gate, up, down, gate_t, up_t
    )
    total = (mine + lax.ppermute(theirs, AXIS, cores).astype(F32)).astype(BF16)
    gate_grad, up_grad, down_grad = grads(
        all_tokens, all_cotangents, gate_delta, up_delta, hidden_t, keeps, total
    )
    sums, down_grad = scatter(total, devices, down_grad)
    return sums[:, :features], sums[:, features:], gate_grad, up_grad, down_grad


def solution(mesh):
    in_specs = (
        P(("group", AXIS), None),
        P(("group", AXIS), None),
        P(None, AXIS),
        P(None, AXIS),
        P(AXIS, None),
        P(None, None, AXIS),
    )
    out_specs = (
        P(("group", AXIS), None),
        P(("group", AXIS), None),
        P(None, ("group", AXIS)),
        P(None, ("group", AXIS)),
        P(("group", AXIS), None),
    )
    body = functools.partial(shards, mesh.shape[AXIS])
    return jax.shard_map(body, mesh=mesh, in_specs=in_specs, out_specs=out_specs, check_vma=False)
```

```python
import functools

import jax
import jax.numpy as jnp
from jax import lax
from jax.experimental import pallas as pl
from jax.experimental.pallas import tpu as pltpu
from jax.sharding import PartitionSpec as P

AXIS = "tensor"
BLOCK = 64
CHUNKS = 4
PARTS = 8
SLOTS = 10
BF16 = jnp.bfloat16
F32 = jnp.float32
MIB = 2**20
VMEM = pl.BlockSpec(memory_space=pltpu.VMEM)


def dot(a, b, ca=1, cb=0):
    return lax.dot_general(a, b, (((ca,), (cb,)), ((), ())), preferred_element_type=F32)


def in_vmem(x):
    return pltpu.with_memory_space_constraint(x, pltpu.VMEM)


def in_hbm(x):
    return pltpu.with_memory_space_constraint(x, pltpu.HBM)


def shape(*dims, dtype=F32):
    return jax.ShapeDtypeStruct(dims, dtype)


def params(mib):
    return pltpu.CompilerParams(vmem_limit_bytes=mib * MIB)


def cost(flops, size):
    return pl.CostEstimate(flops=flops, bytes_accessed=size, transcendentals=0)


def spread(blocks, wide):
    row = lax.broadcasted_iota(jnp.int32, (blocks, wide), 0)
    column = lax.broadcasted_iota(jnp.int32, (blocks, wide), 1)
    return (row == column // BLOCK).astype(BF16)


def keep_lanes(flags, width, transposed):
    return dot(flags, spread(width // BLOCK, width), 1 if transposed else 0, 0)


class Weight:
    def __init__(self, source, target, sems):
        chunks = min(CHUNKS, source.shape[0] // BLOCK)
        rows = source.shape[0] // chunks
        self.target = target
        self.copies = []
        for chunk in range(chunks):
            at = pl.ds(chunk * rows, rows)
            self.copies.append(pltpu.make_async_copy(source.at[at, :], target.at[at, :], sems.at[chunk]))

    def start(self):
        for copy in self.copies:
            copy.start()

    def mask(self, keep, transposed=None):
        keep = keep.astype(BF16)
        blocks = self.target.shape[0] // BLOCK
        each = blocks // len(self.copies)
        for block in range(blocks):
            if block % each == 0:
                self.copies[block // each].wait()
            at = pl.ds(block * BLOCK, BLOCK)
            self.target[at, :] = self.target[at, :] * keep[block : block + 1, :]
            if transposed is not None and block % 2:
                pair = pl.ds((block - 1) * BLOCK, 2 * BLOCK)
                transposed[:, pair] = self.target[pair, :].T


def mask_kernel(flags_ref, gate_hbm, up_hbm, down_hbm, after_ref, *refs):
    targets, transposed, keeps, sems = refs[:3], (*refs[3:5], None), refs[5:8], refs[8]
    weights = [
        Weight(source, target, sems.at[index])
        for index, (source, target) in enumerate(zip((gate_hbm, up_hbm, down_hbm), targets))
    ]
    for weight in weights:
        weight.start()
    for index, (weight, keep_ref) in enumerate(zip(weights, keeps)):
        keep = keep_lanes(flags_ref[index], keep_ref.shape[1], index == 2)
        keep_ref[...] = keep
        weight.mask(keep, transposed[index])


def mask_weights(flags, weights, after):
    hbm = pl.BlockSpec(memory_space=pltpu.HBM)
    return pl.pallas_call(
        mask_kernel,
        out_shape=tuple(pltpu.VMEM(w.shape, BF16) for w in weights)
        + tuple(pltpu.VMEM(w.shape[::-1], BF16) for w in weights[:2])
        + tuple(shape(w.shape[0] // BLOCK, w.shape[1]) for w in weights),
        in_specs=[VMEM] + [hbm] * 3 + [pl.BlockSpec(memory_space=pl.ANY)],
        out_specs=(VMEM,) * 8,
        scratch_shapes=[pltpu.SemaphoreType.DMA((3, CHUNKS))],
        compiler_params=params(8),
        cost_estimate=cost(0, sum(2 * w.size for w in weights)),
        name="mask",
    )(flags, *map(in_hbm, weights), after)


def layer_kernel(pieces, *refs):
    piece_refs = refs[:pieces]
    gate_ref, up_ref, down_ref, gate_t_ref, up_t_ref = refs[pieces : pieces + 5]
    tokens_ref, cotangents_ref, gate_delta_ref, up_delta_ref, hidden_t_ref, mine_ref, theirs_ref = refs[
        pieces + 5 : pieces + 12
    ]
    hidden_ref = refs[pieces + 12]
    features, units = gate_ref.shape
    both = [piece[...] for piece in piece_refs]
    tokens_ref[...] = jnp.concatenate([piece[: piece.shape[0] // 2] for piece in both], 0)
    cotangents_ref[...] = jnp.concatenate([piece[piece.shape[0] // 2 :] for piece in both], 0)
    for start in range(0, units, 256):
        at = pl.ds(start, 256)
        gate = dot(tokens_ref[...], gate_ref[:, at])
        up = dot(tokens_ref[...], up_ref[:, at])
        hidden_grad = dot(cotangents_ref[...], down_ref[at, :], 1, 1)
        sig = jax.nn.sigmoid(gate)
        act = gate * sig
        hidden = act * up
        hidden_ref[:, at] = hidden.astype(BF16)
        hidden_t_ref[at, :] = hidden.T.astype(BF16)
        gate_delta_ref[:, at] = (hidden_grad * up * sig * (1.0 + gate * (1.0 - sig))).astype(BF16)
        up_delta_ref[:, at] = (hidden_grad * act).astype(BF16)
    half = tokens_ref.shape[0] // 2
    for start in range(0, features, 1024):
        at = pl.ds(start, 1024)
        mixed = dot(hidden_ref[...], down_ref[:, at])
        mine_ref[:, at] = mixed[:half]
        theirs_ref[:, at] = mixed[half:].astype(BF16)
        grad = dot(gate_delta_ref[...], gate_t_ref[:, at])
        grad += dot(up_delta_ref[...], up_t_ref[:, at])
        at = pl.ds(features + start, 1024)
        mine_ref[:, at] = grad[:half]
        theirs_ref[:, at] = grad[half:].astype(BF16)


def layer(pieces, gate, up, down, gate_t, up_t):
    rows = sum(piece.shape[0] for piece in pieces) // 2
    features, units = gate.shape
    return pl.pallas_call(
        functools.partial(layer_kernel, len(pieces)),
        out_shape=(
            shape(rows, features, dtype=BF16),
            shape(rows, features, dtype=BF16),
            shape(rows, units, dtype=BF16),
            shape(rows, units, dtype=BF16),
            shape(units, rows, dtype=BF16),
            shape(rows // 2, 2 * features),
            shape(rows // 2, 2 * features, dtype=BF16),
        ),
        in_specs=[VMEM] * (len(pieces) + 5),
        out_specs=(VMEM,) * 7,
        scratch_shapes=[pltpu.VMEM((rows, units), BF16)],
        compiler_params=params(8),
        cost_estimate=cost(12 * rows * features * units, 3 * 2 * features * units),
        name="layer",
    )(*pieces, *map(in_vmem, (gate, up, down, gate_t, up_t)))


def grads_kernel(
    tokens_ref, cotangents_ref, gate_delta_ref, up_delta_ref, hidden_t_ref, keep_g_ref, keep_u_ref, keep_d_ref, after_ref,
    gate_out, up_out, down_out, ring_ref, sems,
):
    features, units = gate_out.shape
    slots, tall, _ = ring_ref.shape
    copies = []

    def slot(rows):
        count = len(copies)
        if count >= slots and count % 2 == 0:
            copies[count - slots].wait()
            copies[count - slots + 1].wait()
        return ring_ref.at[count % slots, pl.ds(0, rows), :]

    def fill(part_ref, columns, grad, keep):
        for block in range(grad.shape[0] // BLOCK):
            at = slice(block * BLOCK, (block + 1) * BLOCK)
            part_ref[at, columns] = (grad[at, :] * keep[block : block + 1, :]).astype(BF16)

    def send(part_ref, out):
        copies.append(pltpu.make_async_copy(part_ref, out, sems.at[len(copies)]))
        copies[-1].start()

    for delta_ref, keep_ref, out in ((gate_delta_ref, keep_g_ref, gate_out), (up_delta_ref, keep_u_ref, up_out)):
        for first in range(0, features, tall):
            at = pl.ds(first, tall)
            part_ref = slot(tall)
            grad = dot(tokens_ref[:, at], delta_ref[...], 0, 0)
            fill(part_ref, slice(0, units), grad, keep_ref[pl.ds(first // BLOCK, tall // BLOCK), :])
            send(part_ref, out.at[at, :])
    flat = min(tall, units)
    wide = min(512, units)
    for first in range(0, units, flat):
        at = pl.ds(first, flat)
        for left in range(0, features, units):
            part_ref = slot(flat)
            for start in range(0, units, wide):
                columns = pl.ds(left + start, wide)
                grad = dot(hidden_t_ref[at, :], cotangents_ref[:, columns])
                keep = keep_d_ref[pl.ds(first // BLOCK, flat // BLOCK), columns]
                fill(part_ref, slice(start, start + wide), grad, keep)
            send(part_ref, down_out.at[at, pl.ds(left, units)])
    for copy in copies[-slots:]:
        copy.wait()


def grads(tokens, cotangents, gate_delta, up_delta, hidden_t, keeps, after):
    rows, features = tokens.shape
    units = hidden_t.shape[0]
    tall = features // PARTS
    hbm = pl.BlockSpec(memory_space=pltpu.HBM)
    shapes = ((features, units), (features, units), (units, features))
    return pl.pallas_call(
        grads_kernel,
        out_shape=tuple(shape(*dims, dtype=BF16) for dims in shapes),
        in_specs=[VMEM] * 8 + [pl.BlockSpec(memory_space=pl.ANY)],
        out_specs=(hbm,) * 3,
        scratch_shapes=[
            pltpu.VMEM((SLOTS, tall, units), BF16),
            pltpu.SemaphoreType.DMA((2 * PARTS + features // min(tall, units),)),
        ],
        compiler_params=params(11),
        cost_estimate=cost(6 * rows * features * units, 3 * 2 * features * units),
        name="grads",
    )(tokens, cotangents, gate_delta, up_delta, hidden_t, *keeps, after)


def across_cores(devices):
    return [(i, i ^ 1) for i in range(devices)]


def across_chips(devices):
    def pairs(offsets):
        return [(i, ((i // 2) ^ offsets[i % 2]) * 2 + i % 2) for i in range(devices)]

    chips = devices // 2
    offsets = [(k + 1, k) if k else (0, 1) for k in range(0, chips, 2)]
    near = len(offsets) // 2
    return [pairs(pair) for pair in offsets[:near] + offsets[:near - 1 : -1]]


def gather(own, devices, after):
    mine = [lax.ppermute(own, AXIS, pairs) for pairs in across_chips(devices)]
    *mine, after = lax.optimization_barrier((*mine, after))
    return mine + [lax.ppermute(piece, AXIS, across_cores(devices)) for piece in mine], after


def scatter(total, devices, after):
    chips = across_chips(devices)
    rows = total.shape[0] // len(chips)
    parts = [lax.ppermute(total[k * rows : (k + 1) * rows], AXIS, pairs) for k, pairs in enumerate(chips)]
    *parts, after = lax.optimization_barrier((*parts, after))
    part = sum(p.astype(F32) for p in parts)
    half = rows // 2
    return (part[:half] + lax.ppermute(part[half:], AXIS, across_cores(devices))).astype(BF16), after


def shards(devices, tokens, cotangent, gate_weight, up_weight, down_weight, block_mask):
    features = tokens.shape[1]
    cores = across_cores(devices)
    here = lax.optimization_barrier(jnp.concatenate([tokens, cotangent], 0))
    flags = jnp.swapaxes(block_mask, 1, 2).astype(BF16)
    other = lax.ppermute(tokens, AXIS, cores), lax.ppermute(cotangent, AXIS, cores)
    here, flags, other = lax.optimization_barrier((here, flags, other))
    rows = tokens.shape[0]
    own = jnp.concatenate([here[:rows], other[0], here[rows:], other[1]], 0)
    gate, up, down, gate_t, up_t, *keeps = mask_weights(flags, (gate_weight, up_weight, down_weight), own)
    pieces, keeps[0] = gather(own, devices, keeps[0])
    all_tokens, all_cotangents, gate_delta, up_delta, hidden_t, mine, theirs = layer(
        pieces, gate, up, down, gate_t, up_t
    )
    total = (mine + lax.ppermute(theirs, AXIS, cores).astype(F32)).astype(BF16)
    gate_grad, up_grad, down_grad = grads(
        all_tokens, all_cotangents, gate_delta, up_delta, hidden_t, keeps, total
    )
    sums, down_grad = scatter(total, devices, down_grad)
    return sums[:, :features], sums[:, features:], gate_grad, up_grad, down_grad


def solution(mesh):
    in_specs = (
        P(("group", AXIS), None),
        P(("group", AXIS), None),
        P(None, AXIS),
        P(None, AXIS),
        P(AXIS, None),
        P(None, None, AXIS),
    )
    out_specs = (
        P(("group", AXIS), None),
        P(("group", AXIS), None),
        P(None, ("group", AXIS)),
        P(None, ("group", AXIS)),
        P(("group", AXIS), None),
    )
    body = functools.partial(shards, mesh.shape[AXIS])
    return jax.shard_map(body, mesh=mesh, in_specs=in_specs, out_specs=out_specs, check_vma=False)
```
